512 devices in a mesh: blk: 128 (over x, y_lo, z), grp: 4 (over y_hi, core).
Axes of the slice: x: 4, y: 4 (y_hi: 2, y_lo: 2; y = y_hi * 2 + y_lo), z: 16, core: 2. Of those that a mesh axis runs over, the one named last changes fastest.
Arguments:
- images: bfloat16 [131072, 1152], P(('blk', 'grp')), may hold values from -0.1796875 to 0.1796875
- texts: bfloat16 [131072, 1152], P(('blk', 'grp')), may hold values from -0.1796875 to 0.1796875
- logit_scale: float32 [1], replicated, may hold values from 8 to 16
- logit_bias: float32 [1], replicated, may hold values from -2 to 1
Outputs:
- image_grad: float32 [131072, 1152], P(('blk', 'grp'))
- text_grad: float32 [131072, 1152], P(('blk', 'grp'))
- row_loss: float32 [131072], P(('blk', 'grp'))
The draws below stay inside these ranges and needn't reach their ends.
All inputs are finite; a program needn't handle non-finite values.
Results may differ from the reference program's by a relative error of at most 0.003.
Values may be sent and summed in bfloat16 or wider, within the bound.
No kernel may reach another device: no remote copies, remote signals or barrier semaphores. Data moves between devices by JAX's collectives and lax.ppermute only.
A program may use at most 64 MiB of HBM per device.

```python
import jax
import jax.numpy as jnp
from jax import lax

D = 1152
BLOCK = 1024
IMAGES = 131072


def steps_of(rng, extent, split, smallest, largest):
    level = 1.0
    for dim, blocks in split:
        steps = jax.random.uniform(jax.random.fold_in(jax.random.fold_in(rng, 6), dim), (blocks,), jnp.float32, smallest / len(split), largest / len(split))
        level = level * jnp.repeat(jnp.exp(steps), extent[dim] // blocks).reshape((-1,) + (1,) * (len(extent) - 1 - dim))
    return level


def normal_values(rng, extent, deviation, reach, cuts=(), kind=jnp.bfloat16):
    values = deviation * jax.random.normal(rng, extent, jnp.float32)
    if cuts:
        values = values * steps_of(rng, extent, cuts, -0.22, 0.18)
    return jnp.clip(values, -reach, reach).astype(kind)


def setup_inputs(seed: int = 0) -> dict:
    key_of = jax.random.split(jax.random.key(seed), 5)
    images = normal_values(key_of[0], (IMAGES, D), 0.0295, 0.1796875, ((0, 512),))
    texts = normal_values(key_of[1], (IMAGES, D), 0.0295, 0.1796875, ((0, 512),))
    logit_scale = jnp.clip(jax.random.uniform(key_of[2], (1,), jnp.float32, 8.0, 16.0), 8.0, 16.0)
    logit_bias = jnp.clip(jax.random.uniform(key_of[3], (1,), jnp.float32, -2.0, 1.0), -2.0, 1.0)
    return dict(images=images, texts=texts, logit_scale=logit_scale, logit_bias=logit_bias)


def pair_terms(image_rows, text_rows, scale, bias, with_labels):
    dots = jnp.dot(image_rows, text_rows.T, preferred_element_type=jnp.float32)
    logits = scale * dots + bias
    count = dots.shape[0]
    if with_labels:
        labels = jnp.where(jnp.eye(count, dtype=jnp.bool_), 1.0, -1.0).astype(jnp.float32)
    else:
        labels = -jnp.ones_like(logits)
    loss = jnp.sum(-jax.nn.log_sigmoid(labels * logits), axis=1)
    coef = (-scale * labels * jax.nn.sigmoid(-labels * logits)).astype(jnp.bfloat16)
    return coef, loss


def reference(images, texts, logit_scale, logit_bias):
    scale = logit_scale[0]
    bias = logit_bias[0]
    blocks = IMAGES // BLOCK
    image_blocks = images.reshape(blocks, BLOCK, D)
    text_blocks = texts.reshape(blocks, BLOCK, D)
    prev_blocks = jnp.roll(text_blocks, 1, axis=0)

    def one_block(items):
        image_rows, own_rows, prev_rows = items
        coef_own, loss_own = pair_terms(image_rows, own_rows, scale, bias, True)
        coef_prev, loss_prev = pair_terms(image_rows, prev_rows, scale, bias, False)
        grad = jnp.dot(coef_own, own_rows, preferred_element_type=jnp.float32) + jnp.dot(coef_prev, prev_rows, preferred_element_type=jnp.float32)
        part_own = jnp.dot(coef_own.T, image_rows, preferred_element_type=jnp.float32)
        part_prev = jnp.dot(coef_prev.T, image_rows, preferred_element_type=jnp.float32)
        return grad, part_own, part_prev, loss_own + loss_prev

    grads, part_own, part_prev, losses = lax.map(one_block, (image_blocks, text_blocks, prev_blocks))
    text_grad = part_own + jnp.roll(part_prev, -1, axis=0)
    return grads.reshape(IMAGES, D), text_grad.reshape(IMAGES, D), losses.reshape(IMAGES)
```

```python
import jax
import jax.numpy as jnp
from jax import lax
from jax.experimental import pallas as pl
from jax.experimental.pallas import tpu as pltpu
from jax.sharding import PartitionSpec as P

AXES = ("blk", "grp")
F32 = jnp.float32
BF16 = jnp.bfloat16
LANES = 128


def send(array, pairs):
    return lax.ppermute(array, AXES, pairs)


def matmul_nt(a, b):
    return lax.dot_general(a, b, (((1,), (1,)), ((), ())), preferred_element_type=F32)


def matmul_nn(a, b):
    return lax.dot_general(a, b, (((1,), (0,)), ((), ())), preferred_element_type=F32)


def matmul_tn(a, b):
    return lax.dot_general(a, b, (((0,), (0,)), ((), ())), preferred_element_type=F32)


def pair_coef(image_rows, text_rows, scale, bias, paired=False, want_loss=True):
    logits = scale * matmul_nt(image_rows, text_rows) + bias
    if paired:
        rows = lax.broadcasted_iota(jnp.int32, logits.shape, 0)
        cols = lax.broadcasted_iota(jnp.int32, logits.shape, 1)
        same = rows == cols
        logits = jnp.where(same, -logits, logits)
    small = jnp.exp(-jnp.abs(logits))
    inverse = 1.0 / (1.0 + small)
    coef = scale * jnp.where(logits >= 0, inverse, small * inverse)
    if paired:
        coef = jnp.where(same, -coef, coef)
    coef = coef.astype(BF16)
    if not want_loss:
        return coef, None
    loss = jnp.maximum(logits, 0.0) + jnp.log1p(small)
    lanes = loss[:, :LANES]
    for i in range(1, loss.shape[1] // LANES):
        lanes = lanes + loss[:, i * LANES : (i + 1) * LANES]
    return coef, lanes


def own_tile(t_ref, b_ref, io, ix, t1, co, cx, lo, lx, x1):
    scale, bias = t_ref[0], b_ref[0]
    coef, lanes = pair_coef(io[...], t1[...], scale, bias, paired=True)
    co[...] = coef
    lo[...] = lanes
    terms = matmul_tn(coef, io[...])
    coef, lanes = pair_coef(ix[...], t1[...], scale, bias)
    cx[...] = coef
    lx[...] = lanes
    x1[...] = terms + matmul_tn(coef, ix[...])


def far_tile(t_ref, b_ref, io, ix, t2, lo, lx, co, cx, lo2, lx2, x2):
    scale, bias = t_ref[0], b_ref[0]
    coef, lanes = pair_coef(io[...], t2[...], scale, bias)
    co[...] = coef
    lo2[...] = lo[...] + lanes
    terms = matmul_tn(coef, io[...])
    coef, lanes = pair_coef(ix[...], t2[...], scale, bias)
    cx[...] = coef
    lx2[...] = lx[...] + lanes
    x2[...] = terms + matmul_tn(coef, ix[...])


def far_text(t_ref, b_ref, jo, jx, t2, x2, out):
    scale, bias = t_ref[0], b_ref[0]
    total = x2[...]
    for rows in (jo, jx):
        coef, _ = pair_coef(rows[...], t2[...], scale, bias, want_loss=False)
        total = total + matmul_tn(coef, rows[...])
    out[...] = total.astype(BF16)


def middle(t_ref, b_ref, jo, jx, t1, x1, io, ix, t2, u1, co1, cx1, co2, cx2, lo, lx,
           x1b, go, gx, lo2, lx2):
    scale, bias = t_ref[0], b_ref[0]
    total = x1[...]
    for rows in (jo, jx):
        coef, _ = pair_coef(rows[...], t1[...], scale, bias, want_loss=False)
        total = total + matmul_tn(coef, rows[...])
    x1b[...] = total
    for rows, c1, c2, l, g, l2 in ((io, co1, co2, lo, go, lo2), (ix, cx1, cx2, lx, gx, lx2)):
        coef, lanes = pair_coef(rows[...], u1[...], scale, bias)
        l2[...] = l[...] + lanes
        g[...] = (
            matmul_nn(c1[...], t1[...]) + matmul_nn(c2[...], t2[...]) + matmul_nn(coef, u1[...])
        )


def last(t_ref, b_ref, io, ix, u2, go, gx, lo, lx, go2, lo2, sent):
    scale, bias = t_ref[0], b_ref[0]
    width = go.shape[1]
    coef, lanes = pair_coef(ix[...], u2[...], scale, bias)
    sent[:, :width] = gx[...] + matmul_nn(coef, u2[...])
    sent[:, width:] = lx[...] + lanes
    coef, lanes = pair_coef(io[...], u2[...], scale, bias)
    go2[...] = go[...] + matmul_nn(coef, u2[...])
    lo2[...] = lo[...] + lanes


def call(kernel, scale, bias, arrays, outs, flops):
    smem = pl.BlockSpec(memory_space=pltpu.SMEM)
    vmem = pl.BlockSpec(memory_space=pltpu.VMEM)
    size = sum(a.size * a.dtype.itemsize for a in (*arrays, *outs))
    return pl.pallas_call(
        kernel,
        in_specs=[smem, smem] + [vmem] * len(arrays),
        out_specs=[vmem] * len(outs),
        out_shape=list(outs),
        compiler_params=pltpu.CompilerParams(vmem_limit_bytes=32 * 2**20),
        cost_estimate=pl.CostEstimate(flops=flops, bytes_accessed=size, transcendentals=0),
    )(scale, bias, *arrays)


def make_per_device(blocks):
    def pairs(to):
        return [
            (k * 4 + h * 2 + c, to(k, h, c))
            for k in range(blocks)
            for h in range(2)
            for c in range(2)
        ]

    def at(k, h, c):
        return (k % blocks) * 4 + h * 2 + c

    next_block = pairs(lambda k, h, c: at(k + 1, h, c))
    prev_block = pairs(lambda k, h, c: at(k - 1, h, c))
    other_half = pairs(lambda k, h, c: at(k, 1 - h, c))
    other_core = pairs(lambda k, h, c: at(k, h, 1 - c))

    def per_device(images, texts, scale, bias):
        rows, width = images.shape
        unit = 2 * rows * rows * width
        f32 = jax.ShapeDtypeStruct((rows, width), F32)
        bf16 = jax.ShapeDtypeStruct((rows, width), BF16)
        coef = jax.ShapeDtypeStruct((rows, rows), BF16)
        lanes = jax.ShapeDtypeStruct((rows, LANES), F32)
        io, t1 = images, texts
        t2 = send(t1, other_half)
        jo = send(io, prev_block)
        u1 = send(t1, next_block)
        ix = send(io, other_core)
        co1, cx1, lo, lx, x1 = call(
            own_tile, scale, bias, (io, ix, t1), (coef, coef, lanes, lanes, f32), 4 * unit
        )
        u2 = send(t2, next_block)
        jx = send(jo, other_core)
        co2, cx2, lo, lx, x2 = call(
            far_tile, scale, bias, (io, ix, t2, lo, lx), (coef, coef, lanes, lanes, f32), 4 * unit
        )
        (x2,) = call(far_text, scale, bias, (jo, jx, t2, x2), (bf16,), 4 * unit)
        back = send(x2, other_half)
        x1, go, gx, lo, lx = call(
            middle,
            scale,
            bias,
            (jo, jx, t1, x1, io, ix, t2, u1, co1, cx1, co2, cx2, lo, lx),
            (f32, f32, f32, lanes, lanes),
            12 * unit,
        )
        sent = jax.ShapeDtypeStruct((rows, width + LANES), F32)
        go, lo, gx = call(
            last, scale, bias, (io, ix, u2, go, gx, lo, lx), (f32, lanes, sent), 4 * unit
        )
        got = send(gx, other_core)
        text_grad = x1 + back.astype(F32)
        image_grad = go + got[:, :width]
        row_loss = jnp.sum(lo + got[:, width:], axis=1)
        return image_grad, text_grad, row_loss

    return per_device


def solution(mesh):
    rows = P(AXES, None)
    return jax.shard_map(
        make_per_device(mesh.shape["blk"]),
        mesh=mesh,
        in_specs=(rows, rows, P(), P()),
        out_specs=(rows, rows, P(AXES)),
        check_vma=False,
    )
```

```python
import jax
import jax.numpy as jnp
from jax import lax
from jax.experimental import pallas as pl
from jax.experimental.pallas import tpu as pltpu
from jax.sharding import PartitionSpec as P

AXES = ("blk", "grp")
F32 = jnp.float32
BF16 = jnp.bfloat16
LANES = 128
RUN = 16
PAD = 16
COST = (1, 1, 1, 1, 1)


def send(array, pairs):
    return lax.ppermute(array, AXES, pairs)


def matmul_nt(a, b):
    return lax.dot_general(a, b, (((1,), (1,)), ((), ())), preferred_element_type=F32)


def matmul_nn(a, b):
    return lax.dot_general(a, b, (((1,), (0,)), ((), ())), preferred_element_type=F32)


def matmul_tn(a, b):
    return lax.dot_general(a, b, (((0,), (0,)), ((), ())), preferred_element_type=F32)


def pair_coef(image_rows, text_rows, scale, bias, paired=False, want_loss=True):
    logits = scale * matmul_nt(image_rows, text_rows) + bias
    if paired:
        rows = lax.broadcasted_iota(jnp.int32, logits.shape, 0)
        cols = lax.broadcasted_iota(jnp.int32, logits.shape, 1)
        same = rows == cols
        logits = jnp.where(same, -logits, logits)
    small = jnp.exp(-jnp.abs(logits))
    inverse = 1.0 / (1.0 + small)
    coef = scale * jnp.where(logits >= 0, inverse, small * inverse)
    if paired:
        coef = jnp.where(same, -coef, coef)
    coef = coef.astype(BF16)
    if not want_loss:
        return coef, None
    loss = jnp.maximum(logits, 0.0) + jnp.log1p(small)
    lanes = loss[:, :LANES]
    for i in range(1, loss.shape[1] // LANES):
        lanes = lanes + loss[:, i * LANES : (i + 1) * LANES]
    return coef, lanes


def own_tile(t_ref, b_ref, io, ix, t1, co, cx, lo, lx, x1):
    scale, bias = t_ref[0], b_ref[0]
    coef, lanes = pair_coef(io[...], t1[...], scale, bias, paired=True)
    co[...] = coef
    lo[...] = lanes
    terms = matmul_tn(coef, io[...])
    coef, lanes = pair_coef(ix[...], t1[...], scale, bias)
    cx[...] = coef
    lx[...] = lanes
    x1[...] = terms + matmul_tn(coef, ix[...])


def main_tiles(t_ref, b_ref, io, ix, jo, jx, t1, t2, u1, co1, cx1, lo, lx, x1,
               x1b, x2, go, gx, lo2):
    scale, bias = t_ref[0], b_ref[0]
    width = t1.shape[1]
    far = None
    near = x1[...]
    for rows in (jo, jx):
        coef, _ = pair_coef(rows[...], t2[...], scale, bias, want_loss=False)
        terms = matmul_tn(coef, rows[...])
        far = terms if far is None else far + terms
        coef, _ = pair_coef(rows[...], t1[...], scale, bias, want_loss=False)
        near = near + matmul_tn(coef, rows[...])
    x1b[...] = near
    for rows, c1, lanes in ((ix, cx1, lx), (io, co1, lo)):
        coef2, more2 = pair_coef(rows[...], t2[...], scale, bias)
        far = far + matmul_tn(coef2, rows[...])
        coef3, more3 = pair_coef(rows[...], u1[...], scale, bias)
        terms = matmul_nn(c1[...], t1[...]) + matmul_nn(coef2, t2[...]) + matmul_nn(coef3, u1[...])
        total = lanes[...] + more2 + more3
        if rows is ix:
            gx[:, :width] = terms.astype(BF16)
            high = total.astype(BF16)
            gx[:, width : width + LANES] = high
            gx[:, width + LANES :] = (total - high.astype(F32)).astype(BF16)
        else:
            go[...] = terms
            lo2[...] = total
    x2[: far.shape[0], :] = far.astype(BF16)
    x2[far.shape[0] :, :] = jnp.zeros((PAD, width), BF16)


def last(t_ref, b_ref, io, u2, u2x, go, lo, go2, lo2):
    scale, bias = t_ref[0], b_ref[0]
    coef, lanes = pair_coef(io[...], u2[...], scale, bias)
    coefx, lanesx = pair_coef(io[...], u2x[...], scale, bias)
    go2[...] = go[...] + matmul_nn(coef, u2[...]) + matmul_nn(coefx, u2x[...])
    lo2[...] = lo[...] + lanes + lanesx


def finish(t_ref, b_ref, go, lo, got, x1, back, image_grad, text_grad, loss):
    width = go.shape[1]
    image_grad[...] = go[...] + got[:, :width].astype(F32)
    text_grad[...] = x1[...] + back[: x1.shape[0], :].astype(F32)
    far = got[:, width : width + LANES].astype(F32) + got[:, width + LANES :].astype(F32)
    loss[...] = jnp.sum((lo[...] + far).T, axis=0, keepdims=True)


def call(kernel, scale, bias, arrays, outs, flops):
    smem = pl.BlockSpec(memory_space=pltpu.SMEM)
    vmem = pl.BlockSpec(memory_space=pltpu.VMEM)
    return pl.pallas_call(
        kernel,
        in_specs=[smem, smem] + [vmem] * len(arrays),
        out_specs=[vmem] * len(outs),
        out_shape=list(outs),
        compiler_params=pltpu.CompilerParams(vmem_limit_bytes=32 * 2**20),
        cost_estimate=pl.CostEstimate(flops=flops, bytes_accessed=0, transcendentals=0),
    )(scale, bias, *arrays)


def make_per_device(blocks):
    def pairs(to):
        return [
            (k * 4 + h * 2 + c, to(k, h, c))
            for k in range(blocks)
            for h in range(2)
            for c in range(2)
        ]

    def at(k, h, c):
        return (k % blocks) * 4 + h * 2 + c

    next_block = pairs(lambda k, h, c: at(k + 1, h ^ (c & (k % RUN == RUN - 1)), c))
    prev_block = pairs(lambda k, h, c: at(k - 1, h ^ (c & (k % RUN == 0)), c))
    other_half = pairs(lambda k, h, c: at(k, 1 - h, c))
    other_core = pairs(lambda k, h, c: at(k, h, 1 - c))

    def per_device(images, texts, scale, bias):
        rows, width = images.shape
        f32 = jax.ShapeDtypeStruct((rows, width), F32)
        padded = jax.ShapeDtypeStruct((rows + PAD, width), BF16)
        coef = jax.ShapeDtypeStruct((rows, rows), BF16)
        lanes = jax.ShapeDtypeStruct((rows, LANES), F32)
        sent = jax.ShapeDtypeStruct((rows, width + 2 * LANES), BF16)
        line = jax.ShapeDtypeStruct((1, rows), F32)
        io, t1 = images, texts
        t2 = send(t1, other_half)
        jo = send(io, prev_block)
        u1 = send(t1, next_block)
        ix = send(io, other_core)
        co1, cx1, lo, lx, x1 = call(
            own_tile, scale, bias, (io, ix, t1), (coef, coef, lanes, lanes, f32), COST[0]
        )
        t2, x1 = lax.optimization_barrier((t2, x1))
        u2 = send(t2, next_block)
        jx = send(jo, other_core)
        x1, x2, go, gx, lo = call(
            main_tiles,
            scale,
            bias,
            (io, ix, jo, jx, t1, t2, u1, co1, cx1, lo, lx, x1),
            (f32, padded, f32, sent, lanes),
            COST[1],
        )
        back = send(x2, other_half)
        got = send(gx, other_core)
        u2x = send(u2, other_core)
        go, lo = call(last, scale, bias, (io, u2, u2x, go, lo), (f32, lanes), COST[3])
        image_grad, text_grad, row_loss = call(
            finish, scale, bias, (go, lo, got, x1, back), (f32, f32, line), COST[4]
        )
        return image_grad, text_grad, row_loss.reshape(rows)

    return per_device


def solution(mesh):
    rows = P(AXES, None)
    return jax.shard_map(
        make_per_device(mesh.shape["blk"]),
        mesh=mesh,
        in_specs=(rows, rows, P(), P()),
        out_specs=(rows, rows, P(AXES)),
        check_vma=False,
    )
```

```python
import jax
import jax.numpy as jnp
from jax import lax
from jax.experimental import pallas as pl
from jax.experimental.pallas import tpu as pltpu
from jax.sharding import PartitionSpec as P

AXES = ("blk", "grp")
F32 = jnp.float32
BF16 = jnp.bfloat16
RUN = 16
SPARE = 16


def send(array, pairs):
    return lax.ppermute(array, AXES, pairs)


def matmul_nt(a, b):
    return lax.dot_general(a, b, (((1,), (1,)), ((), ())), preferred_element_type=F32)


def matmul_nn(a, b):
    return lax.dot_general(a, b, (((1,), (0,)), ((), ())), preferred_element_type=F32)


def matmul_tn(a, b):
    return lax.dot_general(a, b, (((0,), (0,)), ((), ())), preferred_element_type=F32)


def pair_coef(text_rows, image_rows, scale, bias, paired=False, want_loss=True):
    logits = scale * matmul_nt(text_rows, image_rows) + bias
    if paired:
        rows = lax.broadcasted_iota(jnp.int32, logits.shape, 0)
        cols = lax.broadcasted_iota(jnp.int32, logits.shape, 1)
        same = rows == cols
        logits = jnp.where(same, -logits, logits)
    small = jnp.exp(-jnp.abs(logits))
    inverse = 1.0 / (1.0 + small)
    coef = scale * jnp.where(logits >= 0, inverse, small * inverse)
    if paired:
        coef = jnp.where(same, -coef, coef)
    coef = coef.astype(BF16)
    if not want_loss:
        return coef, None
    loss = jnp.maximum(logits, 0.0) + jnp.log1p(small)
    return coef, jnp.sum(loss, axis=0, keepdims=True)


def own_tile(t_ref, b_ref, to, tx, i1, co, cx, loss, y1):
    scale, bias = t_ref[0], b_ref[0]
    coef, loss_o = pair_coef(to[...], i1[...], scale, bias, paired=True)
    co[...] = coef
    terms = matmul_tn(coef, to[...])
    coef, loss_x = pair_coef(tx[...], i1[...], scale, bias)
    cx[...] = coef
    loss[...] = loss_o + loss_x
    y1[...] = terms + matmul_tn(coef, tx[...])


def far_tile(t_ref, b_ref, to, tx, jo, jx, i2, co, cx, out):
    scale, bias = t_ref[0], b_ref[0]
    rows, width = i2.shape
    total = None
    losses = None
    for texts, coefs in ((jo, None), (jx, None), (to, co), (tx, cx)):
        coef, loss = pair_coef(texts[...], i2[...], scale, bias)
        terms = matmul_tn(coef, texts[...])
        total = terms if total is None else total + terms
        losses = loss if losses is None else losses + loss
        if coefs is not None:
            coefs[...] = coef
    out[:rows, :] = total.astype(BF16)
    high = losses.astype(BF16).astype(F32)
    row = lax.broadcasted_iota(jnp.int32, (SPARE, rows), 0)
    split = jnp.where(row == 0, high, jnp.where(row == 1, losses - high, 0.0))
    out[rows:, :] = jnp.zeros((SPARE, width), BF16)
    out[rows:, :rows] = split.astype(BF16)


def middle(t_ref, b_ref, jo, jx, i1, y1, to, tx, i2, v1, co1, cx1, co2, cx2, loss,
           y1b, go, gx, loss2):
    scale, bias = t_ref[0], b_ref[0]
    for texts, c1, c2, out in ((tx, cx1, cx2, gx), (to, co1, co2, go)):
        coef, _ = pair_coef(texts[...], v1[...], scale, bias, want_loss=False)
        terms = (
            matmul_nn(c1[...], i1[...]) + matmul_nn(c2[...], i2[...]) + matmul_nn(coef, v1[...])
        )
        out[...] = terms.astype(out.dtype)
    total = y1[...]
    losses = loss[...]
    for texts in (jo, jx):
        coef, more = pair_coef(texts[...], i1[...], scale, bias)
        total = total + matmul_tn(coef, texts[...])
        losses = losses + more
    y1b[...] = total
    loss2[...] = losses


def last(t_ref, b_ref, to, v2, v2x, go, got, grad):
    scale, bias = t_ref[0], b_ref[0]
    coef, _ = pair_coef(to[...], v2[...], scale, bias, want_loss=False)
    coefx, _ = pair_coef(to[...], v2x[...], scale, bias, want_loss=False)
    grad[...] = (
        go[...] + got[...].astype(F32) + matmul_nn(coef, v2[...]) + matmul_nn(coefx, v2x[...])
    )


def finish(t_ref, b_ref, y1, loss, back, image_grad, row_loss):
    rows = y1.shape[0]
    image_grad[...] = y1[...] + back[:rows, :].astype(F32)
    row_loss[...] = loss[...] + jnp.sum(back[rows:, :rows].astype(F32), axis=0, keepdims=True)


def call(kernel, scale, bias, arrays, outs):
    smem = pl.BlockSpec(memory_space=pltpu.SMEM)
    vmem = pl.BlockSpec(memory_space=pltpu.VMEM)
    return pl.pallas_call(
        kernel,
        in_specs=[smem, smem] + [vmem] * len(arrays),
        out_specs=[vmem] * len(outs),
        out_shape=list(outs),
        compiler_params=pltpu.CompilerParams(vmem_limit_bytes=32 * 2**20),
        cost_estimate=pl.CostEstimate(flops=1, bytes_accessed=0, transcendentals=0),
    )(scale, bias, *arrays)


def make_per_device(blocks):
    def pairs(to):
        return [
            (k * 4 + h * 2 + c, to(k, h, c))
            for k in range(blocks)
            for h in range(2)
            for c in range(2)
        ]

    def at(k, h, c):
        return (k % blocks) * 4 + h * 2 + c

    next_block = pairs(lambda k, h, c: at(k + 1, h ^ (c & (k % RUN == RUN - 1)), c))
    prev_block = pairs(lambda k, h, c: at(k - 1, h ^ (c & (k % RUN == 0)), c))
    other_half = pairs(lambda k, h, c: at(k, 1 - h, c))
    other_core = pairs(lambda k, h, c: at(k, h, 1 - c))

    def per_device(images, texts, scale, bias):
        rows, width = images.shape
        f32 = jax.ShapeDtypeStruct((rows, width), F32)
        bf16 = jax.ShapeDtypeStruct((rows, width), BF16)
        padded = jax.ShapeDtypeStruct((rows + SPARE, width), BF16)
        coef = jax.ShapeDtypeStruct((rows, rows), BF16)
        line = jax.ShapeDtypeStruct((1, rows), F32)
        to, i1 = texts, images
        i2 = send(i1, other_half)
        jo = send(to, next_block)
        v1 = send(i1, prev_block)
        tx = send(to, other_core)
        co1, cx1, loss, y1 = call(
            own_tile, scale, bias, (to, tx, i1), (coef, coef, line, f32)
        )
        i2, v1 = lax.optimization_barrier((i2, v1))
        v2 = send(i2, prev_block)
        jo, y1 = lax.optimization_barrier((jo, y1))
        jx = send(jo, other_core)
        co2, cx2, y2 = call(
            far_tile, scale, bias, (to, tx, jo, jx, i2), (coef, coef, padded)
        )
        back = send(y2, other_half)
        y1, go, gx, loss = call(
            middle,
            scale,
            bias,
            (jo, jx, i1, y1, to, tx, i2, v1, co1, cx1, co2, cx2, loss),
            (f32, f32, bf16, line),
        )
        got = send(gx, other_core)
        v2x = send(v2, other_core)
        (text_grad,) = call(last, scale, bias, (to, v2, v2x, go, got), (f32,))
        y1, text_grad = lax.optimization_barrier((y1, text_grad))
        image_grad, row_loss = call(finish, scale, bias, (y1, loss, back), (f32, line))
        return image_grad, text_grad, row_loss.reshape(rows)

    return per_device


def solution(mesh):
    rows = P(AXES, None)
    return jax.shard_map(
        make_per_device(mesh.shape["blk"]),
        mesh=mesh,
        in_specs=(rows, rows, P(), P()),
        out_specs=(rows, rows, P(AXES)),
        check_vma=False,
    )
```

```python
import jax
import jax.numpy as jnp
from jax import lax
from jax.experimental import pallas as pl
from jax.experimental.pallas import tpu as pltpu
from jax.sharding import PartitionSpec as P

AXES = ("blk", "grp")
F32 = jnp.float32
BF16 = jnp.bfloat16
RUN = 16
SPARE = 16
HOLD = 5 * 10**8


def send(array, pairs):
    return lax.ppermute(array, AXES, pairs)


def matmul_nt(a, b):
    return lax.dot_general(a, b, (((1,), (1,)), ((), ())), preferred_element_type=F32)


def matmul_nn(a, b):
    return lax.dot_general(a, b, (((1,), (0,)), ((), ())), preferred_element_type=F32)


def matmul_tn(a, b):
    return lax.dot_general(a, b, (((0,), (0,)), ((), ())), preferred_element_type=F32)


def pair_coef(text_rows, image_rows, scale, bias, paired=False, want_loss=True):
    logits = scale * matmul_nt(text_rows, image_rows) + bias
    if paired:
        rows = lax.broadcasted_iota(jnp.int32, logits.shape, 0)
        cols = lax.broadcasted_iota(jnp.int32, logits.shape, 1)
        same = rows == cols
        logits = jnp.where(same, -logits, logits)
    small = jnp.exp(-jnp.abs(logits))
    inverse = 1.0 / (1.0 + small)
    coef = scale * jnp.where(logits >= 0, inverse, small * inverse)
    if paired:
        coef = jnp.where(same, -coef, coef)
    coef = coef.astype(BF16)
    if not want_loss:
        return coef, None
    loss = jnp.maximum(logits, 0.0) + jnp.log1p(small)
    return coef, jnp.sum(loss, axis=0, keepdims=True)


def own_tile(t_ref, b_ref, to, tx, i1, co, cx, loss, y1):
    scale, bias = t_ref[0], b_ref[0]
    coef, loss_o = pair_coef(to[...], i1[...], scale, bias, paired=True)
    co[...] = coef
    terms = matmul_tn(coef, to[...])
    coef, loss_x = pair_coef(tx[...], i1[...], scale, bias)
    cx[...] = coef
    loss[...] = loss_o + loss_x
    y1[...] = terms + matmul_tn(coef, tx[...])


def far_tile(t_ref, b_ref, to, tx, jo, jx, i2, co, cx, out):
    scale, bias = t_ref[0], b_ref[0]
    rows, width = i2.shape
    total = None
    losses = None
    for texts, coefs in ((jo, None), (jx, None), (to, co), (tx, cx)):
        coef, loss = pair_coef(texts[...], i2[...], scale, bias)
        terms = matmul_tn(coef, texts[...])
        total = terms if total is None else total + terms
        losses = loss if losses is None else losses + loss
        if coefs is not None:
            coefs[...] = coef
    out[:rows, :] = total.astype(BF16)
    high = losses.astype(BF16).astype(F32)
    row = lax.broadcasted_iota(jnp.int32, (SPARE, rows), 0)
    split = jnp.where(row == 0, high, jnp.where(row == 1, losses - high, 0.0))
    out[rows:, :] = jnp.zeros((SPARE, width), BF16)
    out[rows:, :rows] = split.astype(BF16)


def middle(t_ref, b_ref, jo, jx, i1, y1, to, tx, i2, v1, co1, cx1, co2, cx2, loss,
           y1b, go, gx, loss2):
    scale, bias = t_ref[0], b_ref[0]
    for texts, c1, c2, out in ((tx, cx1, cx2, gx), (to, co1, co2, go)):
        coef, _ = pair_coef(texts[...], v1[...], scale, bias, want_loss=False)
        terms = (
            matmul_nn(c1[...], i1[...]) + matmul_nn(c2[...], i2[...]) + matmul_nn(coef, v1[...])
        )
        out[...] = terms.astype(out.dtype)
    total = y1[...]
    losses = loss[...]
    for texts in (jo, jx):
        coef, more = pair_coef(texts[...], i1[...], scale, bias)
        total = total + matmul_tn(coef, texts[...])
        losses = losses + more
    y1b[...] = total
    loss2[...] = losses


def last(t_ref, b_ref, to, v2, v2x, go, got, grad):
    scale, bias = t_ref[0], b_ref[0]
    coef, _ = pair_coef(to[...], v2[...], scale, bias, want_loss=False)
    coefx, _ = pair_coef(to[...], v2x[...], scale, bias, want_loss=False)
    grad[...] = (
        go[...] + got[...].astype(F32) + matmul_nn(coef, v2[...]) + matmul_nn(coefx, v2x[...])
    )


def finish(t_ref, b_ref, y1, loss, back, image_grad, row_loss):
    rows = y1.shape[0]
    image_grad[...] = y1[...] + back[:rows, :].astype(F32)
    row_loss[...] = loss[...] + jnp.sum(back[rows:, :rows].astype(F32), axis=0, keepdims=True)


def keep(array, cost):
    anywhere = pl.BlockSpec(memory_space=pl.ANY)
    return pl.pallas_call(
        lambda source, target: None,
        in_specs=[anywhere],
        out_specs=anywhere,
        out_shape=jax.ShapeDtypeStruct(array.shape, array.dtype),
        input_output_aliases={0: 0},
        compiler_params=pltpu.CompilerParams(vmem_limit_bytes=2**20),
        cost_estimate=pl.CostEstimate(flops=cost, bytes_accessed=0, transcendentals=0),
    )(array)


def call(kernel, scale, bias, arrays, outs):
    smem = pl.BlockSpec(memory_space=pltpu.SMEM)
    vmem = pl.BlockSpec(memory_space=pltpu.VMEM)
    return pl.pallas_call(
        kernel,
        in_specs=[smem, smem] + [vmem] * len(arrays),
        out_specs=[vmem] * len(outs),
        out_shape=list(outs),
        compiler_params=pltpu.CompilerParams(vmem_limit_bytes=32 * 2**20),
        cost_estimate=pl.CostEstimate(flops=1, bytes_accessed=0, transcendentals=0),
    )(scale, bias, *arrays)


def make_per_device(blocks):
    def pairs(to, of=lambda k: True):
        return [
            (k * 4 + h * 2 + c, to(k, h, c))
            for k in range(blocks)
            if of(k)
            for h in range(2)
            for c in range(2)
        ]

    def at(k, h, c):
        return (k % blocks) * 4 + h * 2 + c

    next_block = pairs(lambda k, h, c: at(k + 1, h ^ (c & (k % RUN == RUN - 1)), c))
    prev_block = pairs(lambda k, h, c: at(k - 1, h ^ (c & (k % RUN == 0)), c))
    inner_prev = pairs(lambda k, h, c: at(k - 1, h, c), lambda k: k % RUN > 0)
    first_prev = pairs(lambda k, h, c: at(k - 1, 1 - h ^ c, c), lambda k: k % RUN == 0)
    other_half = pairs(lambda k, h, c: at(k, 1 - h, c))
    other_core = pairs(lambda k, h, c: at(k, h, 1 - c))

    def per_device(images, texts, scale, bias):
        rows, width = images.shape
        f32 = jax.ShapeDtypeStruct((rows, width), F32)
        bf16 = jax.ShapeDtypeStruct((rows, width), BF16)
        padded = jax.ShapeDtypeStruct((rows + SPARE, width), BF16)
        coef = jax.ShapeDtypeStruct((rows, rows), BF16)
        line = jax.ShapeDtypeStruct((1, rows), F32)
        to, i1 = texts, images
        i2 = send(i1, other_half)
        jo = send(to, next_block)
        v1 = send(i1, prev_block)
        tx = send(to, other_core)
        co1, cx1, loss, y1 = call(
            own_tile, scale, bias, (to, tx, i1), (coef, coef, line, f32)
        )
        v2_line = send(i1, first_prev)
        i2, v1 = lax.optimization_barrier((i2, v1))
        v2 = send(i2, inner_prev)
        jo, y1 = lax.optimization_barrier((jo, y1))
        jx = send(jo, other_core)
        co2, cx2, y2 = call(
            far_tile, scale, bias, (to, tx, jo, jx, i2), (coef, coef, padded)
        )
        back = send(y2, other_half)
        v2_line = keep(v2_line, HOLD)
        y1, v2_line = lax.optimization_barrier((y1, v2_line))
        y1, go, gx, loss = call(
            middle,
            scale,
            bias,
            (jo, jx, i1, y1, to, tx, i2, v1, co1, cx1, co2, cx2, loss),
            (f32, f32, bf16, line),
        )
        got = send(gx, other_core)
        v2 = v2 + v2_line
        v2x = send(v2, other_core)
        (text_grad,) = call(last, scale, bias, (to, v2, v2x, go, got), (f32,))
        y1, text_grad = lax.optimization_barrier((y1, text_grad))
        image_grad, row_loss = call(finish, scale, bias, (y1, loss, back), (f32, line))
        return image_grad, text_grad, row_loss.reshape(rows)

    return per_device


def solution(mesh):
    rows = P(AXES, None)
    return jax.shard_map(
        make_per_device(mesh.shape["blk"]),
        mesh=mesh,
        in_specs=(rows, rows, P(), P()),
        out_specs=(rows, rows, P(AXES)),
        check_vma=False,
    )
```

```python
import jax
import jax.numpy as jnp
from jax import lax
from jax.experimental import pallas as pl
from jax.experimental.pallas import tpu as pltpu
from jax.sharding import PartitionSpec as P

AXES = ("blk", "grp")
F32 = jnp.float32
BF16 = jnp.bfloat16
RUN = 16
SPARE = 16


def send(array, pairs):
    return lax.ppermute(array, AXES, pairs)


def matmul_nt(a, b):
    return lax.dot_general(a, b, (((1,), (1,)), ((), ())), preferred_element_type=F32)


def matmul_nn(a, b):
    return lax.dot_general(a, b, (((1,), (0,)), ((), ())), preferred_element_type=F32)


def matmul_tn(a, b):
    return lax.dot_general(a, b, (((0,), (0,)), ((), ())), preferred_element_type=F32)


def coef_of(dots, scale, bias, paired=False, want_loss=True):
    logits = scale * dots + bias
    if paired:
        rows = lax.broadcasted_iota(jnp.int32, logits.shape, 0)
        cols = lax.broadcasted_iota(jnp.int32, logits.shape, 1)
        same = rows == cols
        logits = jnp.where(same, -logits, logits)
    small = jnp.exp(-jnp.abs(logits))
    inverse = 1.0 / (1.0 + small)
    coef = scale * jnp.where(logits >= 0, inverse, small * inverse)
    if paired:
        coef = jnp.where(same, -coef, coef)
    coef = coef.astype(BF16)
    if not want_loss:
        return coef, None
    loss = jnp.maximum(logits, 0.0) + jnp.log1p(small)
    return coef, jnp.sum(loss, axis=0, keepdims=True)


def own_tile(t_ref, b_ref, to, tx, i1, co, cx, loss, y1):
    scale, bias = t_ref[0], b_ref[0]
    dots = [matmul_nt(texts[...], i1[...]) for texts in (to, tx)]
    coef, loss_o = coef_of(dots[0], scale, bias, paired=True)
    coefx, loss_x = coef_of(dots[1], scale, bias)
    co[...] = coef
    cx[...] = coefx
    loss[...] = loss_o + loss_x
    y1[...] = matmul_tn(coef, to[...]) + matmul_tn(coefx, tx[...])


def far_tile(t_ref, b_ref, to, tx, jo, jx, i2, co, cx, out):
    scale, bias = t_ref[0], b_ref[0]
    rows, width = i2.shape
    held = (jo, jx, to, tx)
    dots = [matmul_nt(texts[...], i2[...]) for texts in held]
    tiles = [coef_of(d, scale, bias) for d in dots]
    co[...] = tiles[2][0]
    cx[...] = tiles[3][0]
    total = sum(matmul_tn(coef, texts[...]) for (coef, _), texts in zip(tiles, held))
    losses = sum(loss for _, loss in tiles)
    out[:rows, :] = total.astype(BF16)
    high = losses.astype(BF16).astype(F32)
    row = lax.broadcasted_iota(jnp.int32, (SPARE, rows), 0)
    split = jnp.where(row == 0, high, jnp.where(row == 1, losses - high, 0.0))
    out[rows:, :] = jnp.zeros((SPARE, width), BF16)
    out[rows:, :rows] = split.astype(BF16)


def middle(t_ref, b_ref, jo, jx, i1, y1, to, tx, i2, v1, co1, cx1, co2, cx2, loss,
           y1b, go, gx, loss2):
    scale, bias = t_ref[0], b_ref[0]
    dots_v = [matmul_nt(texts[...], v1[...]) for texts in (tx, to)]
    dots_j = [matmul_nt(texts[...], i1[...]) for texts in (jo, jx)]
    tiles_v = [coef_of(d, scale, bias, want_loss=False) for d in dots_v]
    for (coef, _), c1, c2, out in zip(tiles_v, (cx1, co1), (cx2, co2), (gx, go)):
        terms = (
            matmul_nn(c1[...], i1[...]) + matmul_nn(c2[...], i2[...]) + matmul_nn(coef, v1[...])
        )
        out[...] = terms.astype(out.dtype)
    tiles_j = [coef_of(d, scale, bias) for d in dots_j]
    y1b[...] = y1[...] + sum(
        matmul_tn(coef, texts[...]) for (coef, _), texts in zip(tiles_j, (jo, jx))
    )
    loss2[...] = loss[...] + sum(more for _, more in tiles_j)


def last(t_ref, b_ref, to, v2, v2x, go, got, grad):
    scale, bias = t_ref[0], b_ref[0]
    dots = [matmul_nt(to[...], images[...]) for images in (v2, v2x)]
    coef, coefx = [coef_of(d, scale, bias, want_loss=False)[0] for d in dots]
    grad[...] = (
        go[...] + got[...].astype(F32) + matmul_nn(coef, v2[...]) + matmul_nn(coefx, v2x[...])
    )


def finish(t_ref, b_ref, y1, loss, back, image_grad, row_loss):
    rows = y1.shape[0]
    image_grad[...] = y1[...] + back[:rows, :].astype(F32)
    row_loss[...] = loss[...] + jnp.sum(back[rows:, :rows].astype(F32), axis=0, keepdims=True)


def call(kernel, scale, bias, arrays, outs):
    smem = pl.BlockSpec(memory_space=pltpu.SMEM)
    vmem = pl.BlockSpec(memory_space=pltpu.VMEM)
    return pl.pallas_call(
        kernel,
        in_specs=[smem, smem] + [vmem] * len(arrays),
        out_specs=[vmem] * len(outs),
        out_shape=list(outs),
        compiler_params=pltpu.CompilerParams(vmem_limit_bytes=32 * 2**20),
        cost_estimate=pl.CostEstimate(flops=1, bytes_accessed=0, transcendentals=0),
    )(scale, bias, *arrays)


def make_per_device(blocks):
    def pairs(to, of=lambda k: True):
        return [
            (k * 4 + h * 2 + c, to(k, h, c))
            for k in range(blocks)
            if of(k)
            for h in range(2)
            for c in range(2)
        ]

    def at(k, h, c):
        return (k % blocks) * 4 + h * 2 + c

    next_block = pairs(lambda k, h, c: at(k + 1, h ^ (c & (k % RUN == RUN - 1)), c))
    prev_block = pairs(lambda k, h, c: at(k - 1, h ^ (c & (k % RUN == 0)), c))
    inner_prev = pairs(lambda k, h, c: at(k - 1, h, c), lambda k: k % RUN > 0)
    first_prev = pairs(lambda k, h, c: at(k - 1, 1 - h ^ c, c), lambda k: k % RUN == 0)
    other_half = pairs(lambda k, h, c: at(k, 1 - h, c))
    other_core = pairs(lambda k, h, c: at(k, h, 1 - c))

    def per_device(images, texts, scale, bias):
        rows, width = images.shape
        f32 = jax.ShapeDtypeStruct((rows, width), F32)
        bf16 = jax.ShapeDtypeStruct((rows, width), BF16)
        padded = jax.ShapeDtypeStruct((rows + SPARE, width), BF16)
        coef = jax.ShapeDtypeStruct((rows, rows), BF16)
        line = jax.ShapeDtypeStruct((1, rows), F32)
        to, i1 = texts, images
        i2 = send(i1, other_half)
        jo = send(to, next_block)
        v1 = send(i1, prev_block)
        tx = send(to, other_core)
        co1, cx1, loss, y1 = call(
            own_tile, scale, bias, (to, tx, i1), (coef, coef, line, f32)
        )
        v2_line = send(i1, first_prev)
        i2, v1 = lax.optimization_barrier((i2, v1))
        v2 = send(i2, inner_prev)
        jo, y1 = lax.optimization_barrier((jo, y1))
        jx = send(jo, other_core)
        co2, cx2, y2 = call(
            far_tile, scale, bias, (to, tx, jo, jx, i2), (coef, coef, padded)
        )
        back = send(y2, other_half)
        y1, go, gx, loss = call(
            middle,
            scale,
            bias,
            (jo, jx, i1, y1, to, tx, i2, v1, co1, cx1, co2, cx2, loss),
            (f32, f32, bf16, line),
        )
        got = send(gx, other_core)
        v2 = v2 + v2_line
        v2x = send(v2, other_core)
        (text_grad,) = call(last, scale, bias, (to, v2, v2x, go, got), (f32,))
        y1, text_grad = lax.optimization_barrier((y1, text_grad))
        image_grad, row_loss = call(finish, scale, bias, (y1, loss, back), (f32, line))
        return image_grad, text_grad, row_loss.reshape(rows)

    return per_device


def solution(mesh):
    rows = P(AXES, None)
    return jax.shard_map(
        make_per_device(mesh.shape["blk"]),
        mesh=mesh,
        in_specs=(rows, rows, P(), P()),
        out_specs=(rows, rows, P(AXES)),
        check_vma=False,
    )
```

```python
import jax
import jax.numpy as jnp
from jax import lax
from jax.experimental import pallas as pl
from jax.experimental.pallas import tpu as pltpu
from jax.sharding import PartitionSpec as P

AXES = ("blk", "grp")
F32 = jnp.float32
BF16 = jnp.bfloat16
RUN = 16
SPARE = 16


def send(array, pairs):
    return lax.ppermute(array, AXES, pairs)


def matmul_nt(a, b):
    return lax.dot_general(a, b, (((1,), (1,)), ((), ())), preferred_element_type=F32)


def matmul_nn(a, b):
    return lax.dot_general(a, b, (((1,), (0,)), ((), ())), preferred_element_type=F32)


def matmul_tn(a, b):
    return lax.dot_general(a, b, (((0,), (0,)), ((), ())), preferred_element_type=F32)


def coef_of(dots, scale, bias, paired=False, want_loss=True):
    logits = scale * dots + bias
    if paired:
        rows = lax.broadcasted_iota(jnp.int32, logits.shape, 0)
        cols = lax.broadcasted_iota(jnp.int32, logits.shape, 1)
        same = rows == cols
        logits = jnp.where(same, -logits, logits)
    small = jnp.exp(-jnp.abs(logits))
    inverse = 1.0 / (1.0 + small)
    coef = scale * jnp.where(logits >= 0, inverse, small * inverse)
    if paired:
        coef = jnp.where(same, -coef, coef)
    coef = coef.astype(BF16)
    if not want_loss:
        return coef, None
    loss = jnp.maximum(logits, 0.0) + jnp.log1p(small)
    return coef, jnp.sum(loss, axis=0, keepdims=True)


def own_tile(t_ref, b_ref, to, i1, co, loss, y1, kept):
    scale, bias = t_ref[0], b_ref[0]
    coef, loss[...] = coef_of(matmul_nt(to[...], i1[...]), scale, bias, paired=True)
    co[...] = coef
    y1[...] = matmul_tn(coef, to[...])
    kept[...] = i1[...]


def far_tile(t_ref, b_ref, to, tx, jo, jx, i2, co, cx, out):
    scale, bias = t_ref[0], b_ref[0]
    rows, width = i2.shape
    held = (jo, jx, to, tx)
    dots = [matmul_nt(texts[...], i2[...]) for texts in held]
    tiles = [coef_of(d, scale, bias) for d in dots]
    co[...] = tiles[2][0]
    cx[...] = tiles[3][0]
    total = sum(matmul_tn(coef, texts[...]) for (coef, _), texts in zip(tiles, held))
    losses = sum(loss for _, loss in tiles)
    out[:rows, :] = total.astype(BF16)
    high = losses.astype(BF16).astype(F32)
    row = lax.broadcasted_iota(jnp.int32, (SPARE, rows), 0)
    split = jnp.where(row == 0, high, jnp.where(row == 1, losses - high, 0.0))
    out[rows:, :] = jnp.zeros((SPARE, width), BF16)
    out[rows:, :rows] = split.astype(BF16)


def middle(t_ref, b_ref, jo, jx, i1, y1, to, tx, i2, v1, co1, co2, cx2, loss,
           y1b, go, gx, loss2):
    scale, bias = t_ref[0], b_ref[0]
    near = (tx, jo, jx)
    dots_i = [matmul_nt(texts[...], i1[...]) for texts in near]
    dots_v = [matmul_nt(texts[...], v1[...]) for texts in (tx, to)]
    tiles_i = [coef_of(d, scale, bias) for d in dots_i]
    tiles_v = [coef_of(d, scale, bias, want_loss=False) for d in dots_v]
    firsts = (tiles_i[0][0], co1[...])
    for (coef, _), c1, c2, out in zip(tiles_v, firsts, (cx2, co2), (gx, go)):
        terms = matmul_nn(c1, i1[...]) + matmul_nn(c2[...], i2[...]) + matmul_nn(coef, v1[...])
        out[...] = terms.astype(out.dtype)
    y1b[...] = y1[...] + sum(
        matmul_tn(coef, texts[...]) for (coef, _), texts in zip(tiles_i, near)
    )
    loss2[...] = loss[...] + sum(more for _, more in tiles_i)


def last(t_ref, b_ref, to, v2, v2x, go, got, grad):
    scale, bias = t_ref[0], b_ref[0]
    dots = [matmul_nt(to[...], images[...]) for images in (v2, v2x)]
    coef, coefx = [coef_of(d, scale, bias, want_loss=False)[0] for d in dots]
    grad[...] = (
        go[...] + got[...].astype(F32) + matmul_nn(coef, v2[...]) + matmul_nn(coefx, v2x[...])
    )


def finish(t_ref, b_ref, y1, loss, back, image_grad, row_loss):
    rows = y1.shape[0]
    image_grad[...] = y1[...] + back[:rows, :].astype(F32)
    row_loss[...] = loss[...] + jnp.sum(back[rows:, :rows].astype(F32), axis=0, keepdims=True)


def call(kernel, scale, bias, arrays, outs):
    smem = pl.BlockSpec(memory_space=pltpu.SMEM)
    vmem = pl.BlockSpec(memory_space=pltpu.VMEM)
    return pl.pallas_call(
        kernel,
        in_specs=[smem, smem] + [vmem] * len(arrays),
        out_specs=[vmem] * len(outs),
        out_shape=list(outs),
        compiler_params=pltpu.CompilerParams(vmem_limit_bytes=32 * 2**20),
        cost_estimate=pl.CostEstimate(flops=1, bytes_accessed=0, transcendentals=0),
    )(scale, bias, *arrays)


def make_per_device(blocks):
    def pairs(to, of=lambda k: True):
        return [
            (k * 4 + h * 2 + c, to(k, h, c))
            for k in range(blocks)
            if of(k)
            for h in range(2)
            for c in range(2)
        ]

    def at(k, h, c):
        return (k % blocks) * 4 + h * 2 + c

    next_block = pairs(lambda k, h, c: at(k + 1, h ^ (c & (k % RUN == RUN - 1)), c))
    prev_block = pairs(lambda k, h, c: at(k - 1, h ^ (c & (k % RUN == 0)), c))
    inner_prev = pairs(lambda k, h, c: at(k - 1, h, c), lambda k: k % RUN > 0)
    first_prev = pairs(lambda k, h, c: at(k - 1, 1 - h ^ c, c), lambda k: k % RUN == 0)
    other_half = pairs(lambda k, h, c: at(k, 1 - h, c))
    other_core = pairs(lambda k, h, c: at(k, h, 1 - c))

    def per_device(images, texts, scale, bias):
        rows, width = images.shape
        f32 = jax.ShapeDtypeStruct((rows, width), F32)
        bf16 = jax.ShapeDtypeStruct((rows, width), BF16)
        padded = jax.ShapeDtypeStruct((rows + SPARE, width), BF16)
        coef = jax.ShapeDtypeStruct((rows, rows), BF16)
        line = jax.ShapeDtypeStruct((1, rows), F32)
        to, i1 = texts, images
        i2 = send(i1, other_half)
        jo = send(to, next_block)
        v1 = send(i1, prev_block)
        tx = send(to, other_core)
        co1, loss, y1, i1 = call(own_tile, scale, bias, (to, i1), (coef, line, f32, bf16))
        v2_line = send(images, first_prev)
        i2, v1, tx = lax.optimization_barrier((i2, v1, tx))
        v2 = send(i2, inner_prev)
        jo, y1 = lax.optimization_barrier((jo, y1))
        jx = send(jo, other_core)
        co2, cx2, y2 = call(
            far_tile, scale, bias, (to, tx, jo, jx, i2), (coef, coef, padded)
        )
        back = send(y2, other_half)
        y1, go, gx, loss = call(
            middle,
            scale,
            bias,
            (jo, jx, i1, y1, to, tx, i2, v1, co1, co2, cx2, loss),
            (f32, f32, bf16, line),
        )
        got = send(gx, other_core)
        v2 = v2 + v2_line
        v2x = send(v2, other_core)
        (text_grad,) = call(last, scale, bias, (to, v2, v2x, go, got), (f32,))
        y1, text_grad = lax.optimization_barrier((y1, text_grad))
        image_grad, row_loss = call(finish, scale, bias, (y1, loss, back), (f32, line))
        return image_grad, text_grad, row_loss.reshape(rows)

    return per_device


def solution(mesh):
    rows = P(AXES, None)
    return jax.shard_map(
        make_per_device(mesh.shape["blk"]),
        mesh=mesh,
        in_specs=(rows, rows, P(), P()),
        out_specs=(rows, rows, P(AXES)),
        check_vma=False,
    )
```
